32 devices in a mesh: row: 4 (over z), col: 2 (over x), clu: 4 (over y, core).
Axes of the slice: x: 2, y: 2, z: 4, core: 2. Of those that a mesh axis runs over, the one named last changes fastest.
Arguments:
- features: bfloat16 [1152, 1024], P(('row', 'col')), may hold values from 0 to 4, as said below
- weights_init: bfloat16 [1152, 1024], P(('row', 'col'), 'clu'), may hold values from 0.001 to 1
Outputs:
- log_assign: float32 [1152, 1024], P(('row', 'col'), 'clu')
The draws below stay inside these ranges and needn't reach their ends.
Inputs may be any that keep to these rules, and one draw needn't show every extreme that they name: `features`: entries are zero or positive; every hit has at least 16 positive entries.
All inputs are finite; a program needn't handle non-finite values.
Results may differ from the reference program's by a relative error of at most 0.0076.
Values may be sent and summed in bfloat16 or wider, within the bound.
A program may use at most 64 MiB of HBM per device.

```python
import math
import jax
import jax.numpy as jnp
from jax import lax

BITS = 1024
CLUSTERS = 1024
ITERS = 2
HITS = 1152


def hit_families(key):
    families = min(64, CLUSTERS // 4)
    member = jax.random.randint(jax.random.fold_in(key, 101), (HITS,), 0, families)
    outlier = jax.random.randint(jax.random.fold_in(key, 102), (HITS,), 0, 8) == 0
    return (families, member, outlier)


def draw_features(key, part):
    families, member, outlier = hit_families(key)
    key = jax.random.fold_in(key, 7)
    subkeys = jax.random.split(key, 6)
    prototype = jax.random.uniform(subkeys[0], (families, BITS)) < 0.5
    flip_rate = jax.random.uniform(subkeys[1], (families,), minval=0.01, maxval=0.12)
    flipped = jax.random.uniform(subkeys[2], (HITS, BITS)) < flip_rate[member][:, None]
    family_bits = jnp.logical_xor(prototype[member], flipped)
    sparse_bits = jax.random.uniform(subkeys[5], (HITS, BITS)) < 0.1
    present = jnp.where(outlier[:, None], sparse_bits, family_bits)
    column = jnp.arange(BITS)[None, :] % 64
    row_slot = jnp.arange(HITS)[:, None] % 64
    present = jnp.logical_or(present, column == row_slot)
    magnitude = jax.random.uniform(subkeys[4], (HITS, BITS), minval=0.5, maxval=2.0)
    return jnp.where(present, magnitude, 0.0).astype(jnp.bfloat16)


def draw_weights_init(key, part):
    families, member, outlier = hit_families(key)
    key = jax.random.fold_in(key, 11)
    subkeys = jax.random.split(key, 2)
    per = CLUSTERS // families
    cluster_family = jnp.arange(CLUSTERS) // per
    own = member[:, None] == cluster_family[None, :]
    strong = jnp.exp(jax.random.uniform(subkeys[0], (HITS, CLUSTERS), minval=math.log(0.5), maxval=math.log(0.98)))
    faint = jnp.exp(jax.random.uniform(subkeys[1], (HITS, CLUSTERS), minval=math.log(0.0011), maxval=math.log(0.004)))
    return jnp.where(own, strong, faint).astype(jnp.bfloat16)


def setup_inputs(seed: int = 0) -> dict:
    splits = jax.random.split(jax.random.key(seed), 3)
    return {
        "features": draw_features(jax.random.fold_in(splits[2], 71), 0),
        "weights_init": draw_weights_init(jax.random.fold_in(splits[2], 71), 0),
    }


BETA = 320.0


def squared_norms(rows):
    widened = rows.astype(jnp.float32)
    return jnp.sum(widened * widened, axis=1)


def reference(features, weights_init):
    count = features.shape[0]
    block = math.gcd(count, 512)
    norms = squared_norms(features)
    starts = jnp.arange(count // block, dtype=jnp.int32) * block
    assign = weights_init
    log_assign = jnp.zeros(weights_init.shape, jnp.float32)
    for step in range(ITERS):
        def block_products(start, current=assign):
            rows = lax.dynamic_slice_in_dim(features, start.astype(jnp.int32), block, 0)
            row_norms = lax.dynamic_slice_in_dim(norms, start.astype(jnp.int32), block, 0)
            gram = jnp.dot(rows, features.T, preferred_element_type=jnp.float32)
            kernel = (gram / (row_norms[:, None] + norms[None, :] - gram)).astype(jnp.bfloat16)
            return jnp.dot(kernel, current, preferred_element_type=jnp.float32)

        products = lax.map(block_products, starts).reshape(count, assign.shape[1])
        widened = assign.astype(jnp.float32)
        size_sum = jnp.maximum(jnp.sum(widened, axis=0), 1.0)
        within = jnp.sum(widened * products, axis=0)
        score = BETA * (2.0 * products / size_sum[None, :] - (within / (size_sum * size_sum))[None, :])
        top = jnp.max(score, axis=1, keepdims=True)
        total = jnp.sum(jnp.exp(score - top), axis=1, keepdims=True)
        log_assign = score - top - jnp.log(total)
        assign = jnp.exp(log_assign).astype(jnp.bfloat16)
    return log_assign
```

```python
import functools

import jax
import jax.numpy as jnp
from jax import lax
from jax.experimental import pallas as pl
from jax.experimental.pallas import tpu as pltpu
from jax.sharding import PartitionSpec as P

ITERS = 2


BETA = 320.0


def squared_norms(rows):
    widened = rows.astype(jnp.float32)
    return jnp.sum(widened * widened, axis=1)


def tanimoto(left, left_norms, right):
    gram = jnp.dot(left, right.T, preferred_element_type=jnp.float32)
    return (gram / (left_norms[:, None] + squared_norms(right)[None, :] - gram)).astype(
        jnp.bfloat16
    )


def on_device(features, weights_init):
    references = lax.all_gather(features, "row", axis=0, tiled=True)
    ref_norms = squared_norms(references)
    assign = weights_init
    log_assign = jnp.zeros(weights_init.shape, jnp.float32)
    for step in range(ITERS):
        moving = assign
        kernel_tile = tanimoto(
            references, ref_norms, lax.all_gather(features, "col", axis=0, tiled=True)
        )
        wide_partial = jnp.dot(
            kernel_tile,
            lax.all_gather(moving, "col", axis=0, tiled=True),
            preferred_element_type=jnp.float32,
        )
        products = lax.psum_scatter(wide_partial, "row", scatter_dimension=0, tiled=True)
        widened = assign.astype(jnp.float32)
        local_within = jnp.sum(widened * products, axis=0)
        size_sum, within = lax.psum((jnp.sum(widened, axis=0), local_within), ("row", "col"))
        size_sum = jnp.maximum(size_sum, 1.0)
        score = BETA * (
            2.0 * products / size_sum[None, :] - (within / (size_sum * size_sum))[None, :]
        )
        top = lax.pmax(jnp.max(score, axis=1), "clu")
        total = lax.psum(jnp.sum(jnp.exp(score - top[:, None]), axis=1), "clu")
        log_assign = score - top[:, None] - jnp.log(total)[:, None]
        assign = jnp.exp(log_assign).astype(jnp.bfloat16)
    return log_assign


def block_order(rows, cols):
    near = [dz for dz in range(1, rows) if dz in (1, rows - 1)]
    far = [dz for dz in range(1, rows) if dz not in near]
    order = [(0, 0)] + [(0, dz) for dz in near]
    order += [(dx, 0) for dx in range(1, cols)]
    order += [(0, dz) for dz in far]
    order += [(dx, dz) for dz in near + far for dx in range(1, cols)]
    return order


def strips_after(blocks, block, total):
    done, plan = 0, {}
    for n in range(1, blocks + 1):
        ready = n * block
        grain = 256 if n < blocks - 1 else 128
        end = total if n == blocks else ready // grain * grain
        if end > done:
            plan[n] = (done, end)
            done = end
    return plan


def tiles_of(lo, hi, size=256):
    return [(a, min(a + size, hi)) for a in range(lo, hi, size)]


def kernel(
    rows,
    cols,
    feat,
    weights,
    out,
    f_all,
    w_all,
    k_all,
    a_all,
    p_all,
    norm_col,
    norm_row,
    stats,
    stats_own,
    local_sem,
    f_send,
    f_recv,
    fx_send,
    fz_send,
    w_send,
    wx_send,
    w_recv,
    s_send,
    s_recv,
):
    block = feat.shape[0]
    total, part = w_all.shape
    quarter = f_all.shape[2]
    blocks = rows * cols
    z, x, q = lax.axis_index("row"), lax.axis_index("col"), lax.axis_index("clu")
    y, c = q // 2, q % 2
    order = block_order(rows, cols)
    place = {b: i for i, b in enumerate(order)}

    def row_peer(d):
        return {"row": lax.rem(z + d, rows)}

    def col_peer(d):
        return {"col": lax.rem(x + d, cols)}

    flip = [None, {"clu": y * 2 + 1 - c}, {"clu": (1 - y) * 2 + c}, {"clu": (1 - y) * 2 + 1 - c}]

    def span(i):
        return pl.ds(i * block, block)

    def quarter_of(r):
        index = q if r == 0 else flip[r]["clu"]
        return feat.at[:, pl.ds(pl.multiple_of(index * quarter, quarter), quarter)]

    own = []
    for r in range(4):
        own.append(
            pltpu.make_async_copy(quarter_of(r), f_all.at[r, span(0)], local_sem.at[r])
        )
    own.append(pltpu.make_async_copy(weights, w_all.at[span(0)], local_sem.at[4]))
    for copy in own:
        copy.start()

    barrier = pltpu.get_barrier_semaphore()
    peers = [row_peer(d) for d in range(1, rows)] + [col_peer(d) for d in range(1, cols)] + flip[1:]
    for peer in peers:
        pl.semaphore_signal(barrier, inc=1, device_id=peer, device_id_type=pl.DeviceIdType.MESH)
    pl.semaphore_wait(barrier, len(peers))

    sent = []

    def send(src, dst, send_sem, recv_sem, peer):
        copy = pltpu.make_async_remote_copy(
            src_ref=src,
            dst_ref=dst,
            send_sem=send_sem,
            recv_sem=recv_sem,
            device_id=peer,
            device_id_type=pl.DeviceIdType.MESH,
        )
        copy.start()
        sent.append(copy)

    def arrived(dst, recv_sem):
        pltpu.make_async_copy(dst, dst, recv_sem).wait()

    def send_f_col(b, src):
        for d in range(1, cols):
            i = place[(cols - d, b[1])]
            send(src, f_all.at[0, span(i)], fx_send.at[d, b[1]], f_recv.at[0, i], col_peer(d))

    def send_w_col(b, src):
        for d in range(1, cols):
            i = place[(cols - d, b[1])]
            send(src, w_all.at[span(i)], wx_send.at[d, b[1]], w_recv.at[i], col_peer(d))

    send_f_col((0, 0), quarter_of(0))
    for b in order[1:]:
        if b[0] == 0:
            i = place[(0, rows - b[1])]
            send(quarter_of(0), f_all.at[0, span(i)], fz_send.at[b[1]], f_recv.at[0, i], row_peer(b[1]))
    for b in order[1:]:
        if b[0] == 0:
            i = place[(0, rows - b[1])]
            send(weights, w_all.at[span(i)], w_send.at[b[1]], w_recv.at[i], row_peer(b[1]))

    for i, b in enumerate(order):
        if i == 0:
            continue
        here = f_all.at[0, span(i)]
        arrived(here, f_recv.at[0, i])
        if b[0] == 0:
            send_f_col(b, here)
        send(here, f_all.at[2, span(i)], f_send.at[2, i], f_recv.at[2, i], flip[2])
        send(here, f_all.at[1, span(i)], f_send.at[1, i], f_recv.at[1, i], flip[1])
        if i == rows:
            send_w_col((0, 0), weights)
    for i, b in enumerate(order):
        if i > 0 and b[0] == 0:
            here = w_all.at[span(i)]
            arrived(here, w_recv.at[i])
            send_w_col(b, here)

    def gram(a, b):
        acc = None
        for r in range(4):
            g = lax.dot_general(
                f_all[r, a[0] : a[1]],
                f_all[r, b[0] : b[1]],
                (((1,), (1,)), ((), ())),
                preferred_element_type=jnp.float32,
            )
            acc = g if acc is None else acc + g
        return acc

    def ratio(g, a, b):
        under = norm_col[a[0] : a[1], :] + norm_row[:, b[0] : b[1]] - g
        return (g / under).astype(jnp.bfloat16)

    def strip(lo, hi):
        for t in tiles_of(lo, hi):
            g = gram(t, t)
            eye = lax.broadcasted_iota(jnp.int32, g.shape, 0) == lax.broadcasted_iota(
                jnp.int32, g.shape, 1
            )
            diag = jnp.where(eye, g, 0.0)
            norm_col[t[0] : t[1], :] = jnp.sum(diag, axis=1, keepdims=True)
            norm_row[:, t[0] : t[1]] = jnp.sum(diag, axis=0, keepdims=True)
            k_all[t[0] : t[1], t[0] : t[1]] = ratio(g, t, t)
            for u in tiles_of(0, t[0]):
                k_all[u[0] : u[1], t[0] : t[1]] = ratio(gram(u, t), u, t)
                k_all[t[0] : t[1], u[0] : u[1]] = ratio(gram(t, u), t, u)

    plan = strips_after(blocks, block, total)
    for copy in own[:4]:
        copy.wait()

    def finish(i):
        for r in (1, 3):
            if i > 0:
                arrived(f_all.at[r, span(i)], f_recv.at[r, i])
        if i + 1 in plan:
            strip(*plan[i + 1])

    for i in range(1, blocks):
        here = f_all.at[2, span(i)]
        arrived(here, f_recv.at[2, i])
        send(here, f_all.at[3, span(i)], f_send.at[3, i], f_recv.at[3, i], flip[1])
        finish(i - 1)
    finish(blocks - 1)

    own[4].wait()
    for i, b in enumerate(order):
        if b[0] > 0:
            arrived(w_all.at[span(i)], w_recv.at[i])
    for t in tiles_of(0, total, 128):
        a_all[:, t[0] : t[1]] = w_all[t[0] : t[1], :].astype(jnp.float32).T.astype(jnp.bfloat16)

    wide = tiles_of(0, total, 384)
    for step in range(ITERS):
        last = step == ITERS - 1
        size = jnp.zeros((part, 1), jnp.float32)
        within = jnp.zeros((part, 1), jnp.float32)
        for t in wide:
            p = jnp.dot(a_all[...], k_all[:, t[0] : t[1]], preferred_element_type=jnp.float32)
            p_all[:, t[0] : t[1]] = p
            a = a_all[:, t[0] : t[1]].astype(jnp.float32)
            size += jnp.sum(a, axis=1, keepdims=True)
            within += jnp.sum(a * p, axis=1, keepdims=True)
        size = jnp.maximum(size, 1.0)
        scale = (2.0 * BETA) / size
        shift = BETA * (within / (size * size))
        span_all = [(0, -(-block // 128) * 128)] if last else wide
        end = span_all[-1][1]
        for t in span_all:
            score = p_all[:, t[0] : t[1]] * scale - shift
            p_all[:, t[0] : t[1]] = score
            top = jnp.max(score, axis=0, keepdims=True)
            stats_own[step, 0:1, t[0] : t[1]] = top
            stats_own[step, 1:2, t[0] : t[1]] = jnp.sum(jnp.exp(score - top), axis=0, keepdims=True)
        mine = stats_own.at[step, :, pl.ds(0, end)]
        for r in (2, 3, 1):
            send(
                mine,
                stats.at[step, r - 1, :, pl.ds(0, end)],
                s_send.at[step, r - 1],
                s_recv.at[step, r - 1],
                flip[r],
            )
        for r in (1, 2, 3):
            arrived(stats.at[step, r - 1, :, pl.ds(0, end)], s_recv.at[step, r - 1])
        for t in span_all:
            cut = slice(t[0], t[1])
            tops = [stats_own[step, 0:1, cut]] + [stats[step, r, 0:1, cut] for r in range(3)]
            sums = [stats_own[step, 1:2, cut]] + [stats[step, r, 1:2, cut] for r in range(3)]
            top = functools.reduce(jnp.maximum, tops)
            sum_all = sum(s * jnp.exp(m - top) for m, s in zip(tops, sums))
            log_assign = p_all[:, cut] - top - jnp.log(sum_all)
            if last:
                out[...] = log_assign.T[:block, :]
            else:
                a_all[:, cut] = jnp.exp(log_assign).astype(jnp.bfloat16)

    for copy in sent:
        copy.wait_send()


def fused(rows, cols, features, weights_init):
    block, bits = features.shape
    part = weights_init.shape[1]
    blocks = rows * cols
    total = block * blocks
    dma = pltpu.SemaphoreType.DMA
    flops = 2 * total * total * (bits + ITERS * part)
    return pl.pallas_call(
        functools.partial(kernel, rows, cols),
        out_shape=jax.ShapeDtypeStruct((block, part), jnp.float32),
        in_specs=[pl.BlockSpec(memory_space=pl.ANY)] * 2,
        out_specs=pl.BlockSpec(memory_space=pltpu.VMEM),
        scratch_shapes=[
            pltpu.VMEM((4, total, bits // 4), jnp.bfloat16),
            pltpu.VMEM((total, part), jnp.bfloat16),
            pltpu.VMEM((total, total), jnp.bfloat16),
            pltpu.VMEM((part, total), jnp.bfloat16),
            pltpu.VMEM((part, total), jnp.float32),
            pltpu.VMEM((total, 1), jnp.float32),
            pltpu.VMEM((1, total), jnp.float32),
            pltpu.VMEM((ITERS, 3, 2, total), jnp.float32),
            pltpu.VMEM((ITERS, 2, total), jnp.float32),
            dma((5,)),
            dma((4, blocks)),
            dma((4, blocks)),
            dma((cols, rows)),
            dma((rows,)),
            dma((rows,)),
            dma((cols, rows)),
            dma((blocks,)),
            dma((ITERS, 3)),
            dma((ITERS, 3)),
        ],
        compiler_params=pltpu.CompilerParams(
            collective_id=0, has_side_effects=True, vmem_limit_bytes=48 * 1024 * 1024
        ),
        cost_estimate=pl.CostEstimate(
            flops=flops, bytes_accessed=4 * block * (bits + part), transcendentals=total * part
        ),
    )(features, weights_init)


def fits(rows, cols, clus, hits, bits, clusters):
    blocks = rows * cols
    if clus != 4 or hits % blocks or hits % 128 or bits % 512 or clusters % 512:
        return False
    block = hits // blocks
    held = 2 * hits * (bits + hits) + 10 * hits * (clusters // clus)
    return block % 16 == 0 and rows > 1 and cols > 1 and held <= 16 * 1024 * 1024


def solution(mesh):
    placed = (P(("row", "col"), None), P(("row", "col"), "clu"))
    rows, cols, clus = (mesh.shape[a] for a in ("row", "col", "clu"))

    def whole(features, weights_init):
        hits, bits = features.shape
        ok = fits(rows, cols, clus, hits, bits, weights_init.shape[1])
        body = functools.partial(fused, rows, cols) if ok else on_device
        return jax.shard_map(
            body, mesh=mesh, in_specs=placed, out_specs=P(("row", "col"), "clu"), check_vma=False
        )(features, weights_init)

    return whole
```

```python
import functools

import jax
import jax.numpy as jnp
from jax import lax
from jax.experimental import pallas as pl
from jax.experimental.pallas import tpu as pltpu
from jax.sharding import PartitionSpec as P

ITERS = 2


BETA = 320.0


def squared_norms(rows):
    widened = rows.astype(jnp.float32)
    return jnp.sum(widened * widened, axis=1)


def tanimoto(left, left_norms, right):
    gram = jnp.dot(left, right.T, preferred_element_type=jnp.float32)
    return (gram / (left_norms[:, None] + squared_norms(right)[None, :] - gram)).astype(
        jnp.bfloat16
    )


def on_device(features, weights_init):
    references = lax.all_gather(features, "row", axis=0, tiled=True)
    ref_norms = squared_norms(references)
    assign = weights_init
    log_assign = jnp.zeros(weights_init.shape, jnp.float32)
    for step in range(ITERS):
        moving = assign
        kernel_tile = tanimoto(
            references, ref_norms, lax.all_gather(features, "col", axis=0, tiled=True)
        )
        wide_partial = jnp.dot(
            kernel_tile,
            lax.all_gather(moving, "col", axis=0, tiled=True),
            preferred_element_type=jnp.float32,
        )
        products = lax.psum_scatter(wide_partial, "row", scatter_dimension=0, tiled=True)
        widened = assign.astype(jnp.float32)
        local_within = jnp.sum(widened * products, axis=0)
        size_sum, within = lax.psum((jnp.sum(widened, axis=0), local_within), ("row", "col"))
        size_sum = jnp.maximum(size_sum, 1.0)
        score = BETA * (
            2.0 * products / size_sum[None, :] - (within / (size_sum * size_sum))[None, :]
        )
        top = lax.pmax(jnp.max(score, axis=1), "clu")
        total = lax.psum(jnp.sum(jnp.exp(score - top[:, None]), axis=1), "clu")
        log_assign = score - top[:, None] - jnp.log(total)[:, None]
        assign = jnp.exp(log_assign).astype(jnp.bfloat16)
    return log_assign


def block_order(rows, cols):
    near = [dz for dz in range(1, rows) if dz in (1, rows - 1)]
    far = [dz for dz in range(1, rows) if dz not in near]
    order = [(0, 0)] + [(0, dz) for dz in near]
    order += [(dx, 0) for dx in range(1, cols)]
    order += [(0, dz) for dz in far]
    order += [(dx, dz) for dz in near + far for dx in range(1, cols)]
    return order


def strips_after(blocks, block, total):
    done, plan = 0, {}
    for n in range(1, blocks + 1):
        ready = n * block
        grain = 256 if n < blocks - 1 else 128
        end = total if n == blocks else ready // grain * grain
        if end > done:
            plan[n] = (done, end)
            done = end
    return plan


def tiles_of(lo, hi, size=256):
    return [(a, min(a + size, hi)) for a in range(lo, hi, size)]


def kernel(
    rows,
    cols,
    feat,
    weights,
    out,
    f_all,
    w_all,
    k_all,
    a_all,
    p_all,
    norm_col,
    norm_row,
    stats,
    stats_own,
    local_sem,
    f_send,
    f_recv,
    fx_send,
    fz_send,
    w_send,
    wx_send,
    w_recv,
    s_send,
    s_recv,
):
    block = feat.shape[0]
    total, part = w_all.shape
    quarter = f_all.shape[2]
    blocks = rows * cols
    z, x, q = lax.axis_index("row"), lax.axis_index("col"), lax.axis_index("clu")
    y, c = q // 2, q % 2
    order = block_order(rows, cols)
    place = {b: i for i, b in enumerate(order)}

    def row_peer(d):
        return {"row": lax.rem(z + d, rows)}

    def col_peer(d):
        return {"col": lax.rem(x + d, cols)}

    flip = [None, {"clu": y * 2 + 1 - c}, {"clu": (1 - y) * 2 + c}, {"clu": (1 - y) * 2 + 1 - c}]

    def span(i):
        return pl.ds(i * block, block)

    def quarter_of(r):
        index = q if r == 0 else flip[r]["clu"]
        return feat.at[:, pl.ds(pl.multiple_of(index * quarter, quarter), quarter)]

    own = []
    for r in range(4):
        own.append(
            pltpu.make_async_copy(quarter_of(r), f_all.at[r, span(0)], local_sem.at[r])
        )
    own.append(pltpu.make_async_copy(weights, w_all.at[span(0)], local_sem.at[4]))
    for copy in own:
        copy.start()

    barrier = pltpu.get_barrier_semaphore()
    peers = [row_peer(d) for d in range(1, rows)] + [col_peer(d) for d in range(1, cols)] + flip[1:]
    for peer in peers:
        pl.semaphore_signal(barrier, inc=1, device_id=peer, device_id_type=pl.DeviceIdType.MESH)
    pl.semaphore_wait(barrier, len(peers))

    sent = []

    def send(src, dst, send_sem, recv_sem, peer):
        copy = pltpu.make_async_remote_copy(
            src_ref=src,
            dst_ref=dst,
            send_sem=send_sem,
            recv_sem=recv_sem,
            device_id=peer,
            device_id_type=pl.DeviceIdType.MESH,
        )
        copy.start()
        sent.append(copy)

    def arrived(dst, recv_sem):
        pltpu.make_async_copy(dst, dst, recv_sem).wait()

    def send_f_col(b, src):
        for d in range(1, cols):
            i = place[(cols - d, b[1])]
            send(src, f_all.at[0, span(i)], fx_send.at[d, b[1]], f_recv.at[0, i], col_peer(d))

    def send_w_col(b, src):
        for d in range(1, cols):
            i = place[(cols - d, b[1])]
            send(src, w_all.at[span(i)], wx_send.at[d, b[1]], w_recv.at[i], col_peer(d))

    send_f_col((0, 0), quarter_of(0))
    for b in order[1:]:
        if b[0] == 0:
            i = place[(0, rows - b[1])]
            send(quarter_of(0), f_all.at[0, span(i)], fz_send.at[b[1]], f_recv.at[0, i], row_peer(b[1]))

    def send_w_row(near):
        for dz in range(1, rows):
            if (dz in (1, rows - 1)) == near:
                j = place[(0, rows - dz)]
                send(weights, w_all.at[span(j)], w_send.at[dz], w_recv.at[j], row_peer(dz))

    for i, b in enumerate(order):
        here = f_all.at[0, span(i)]
        if i > 0:
            arrived(here, f_recv.at[0, i])
            if b[0] == 0:
                send_f_col(b, here)
            send(here, f_all.at[2, span(i)], f_send.at[2, i], f_recv.at[2, i], flip[2])
            send(here, f_all.at[1, span(i)], f_send.at[1, i], f_recv.at[1, i], flip[1])
        if i == 1:
            send_w_row(True)
        if i == 2:
            send_w_row(False)
        if i == 0:
            send_w_col((0, 0), weights)

    def pass_weights():
        for i, b in enumerate(order):
            if i > 0 and b[0] == 0:
                here = w_all.at[span(i)]
                arrived(here, w_recv.at[i])
                send_w_col(b, here)

    def gram(a, b):
        acc = None
        for r in range(4):
            g = lax.dot_general(
                f_all[r, a[0] : a[1]],
                f_all[r, b[0] : b[1]],
                (((1,), (1,)), ((), ())),
                preferred_element_type=jnp.float32,
            )
            acc = g if acc is None else acc + g
        return acc

    def ratio(g, a, b):
        under = norm_col[a[0] : a[1], :] + norm_row[:, b[0] : b[1]] - g
        return (g / under).astype(jnp.bfloat16)

    def strip(lo, hi):
        for t in tiles_of(lo, hi):
            g = gram(t, t)
            eye = lax.broadcasted_iota(jnp.int32, g.shape, 0) == lax.broadcasted_iota(
                jnp.int32, g.shape, 1
            )
            diag = jnp.where(eye, g, 0.0)
            norm_col[t[0] : t[1], :] = jnp.sum(diag, axis=1, keepdims=True)
            norm_row[:, t[0] : t[1]] = jnp.sum(diag, axis=0, keepdims=True)
            k_all[t[0] : t[1], t[0] : t[1]] = ratio(g, t, t)
            for u in tiles_of(0, t[0]):
                k_all[u[0] : u[1], t[0] : t[1]] = ratio(gram(u, t), u, t)
                k_all[t[0] : t[1], u[0] : u[1]] = ratio(gram(t, u), t, u)

    plan = strips_after(blocks, block, total)
    for copy in own[:4]:
        copy.wait()

    def finish(i):
        for r in (1, 3):
            if i > 0:
                arrived(f_all.at[r, span(i)], f_recv.at[r, i])
        if i + 1 in plan:
            strip(*plan[i + 1])

    for i in range(1, blocks):
        here = f_all.at[2, span(i)]
        arrived(here, f_recv.at[2, i])
        send(here, f_all.at[3, span(i)], f_send.at[3, i], f_recv.at[3, i], flip[1])
        finish(i - 1)
        if i == min(3, blocks - 1):
            pass_weights()
    finish(blocks - 1)

    own[4].wait()
    for i, b in enumerate(order):
        if b[0] > 0:
            arrived(w_all.at[span(i)], w_recv.at[i])
    for t in tiles_of(0, total, 128):
        a_all[:, t[0] : t[1]] = w_all[t[0] : t[1], :].astype(jnp.float32).T.astype(jnp.bfloat16)

    wide = tiles_of(0, total, 384)
    for step in range(ITERS):
        last = step == ITERS - 1
        size = jnp.zeros((part, 1), jnp.float32)
        within = jnp.zeros((part, 1), jnp.float32)
        for t in wide:
            p = jnp.dot(a_all[...], k_all[:, t[0] : t[1]], preferred_element_type=jnp.float32)
            p_all[:, t[0] : t[1]] = p
            a = a_all[:, t[0] : t[1]].astype(jnp.float32)
            size += jnp.sum(a, axis=1, keepdims=True)
            within += jnp.sum(a * p, axis=1, keepdims=True)
        size = jnp.maximum(size, 1.0)
        scale = (2.0 * BETA) / size
        shift = BETA * (within / (size * size))
        span_all = [(0, -(-block // 128) * 128)] if last else wide
        end = span_all[-1][1]
        for t in span_all:
            score = p_all[:, t[0] : t[1]] * scale - shift
            p_all[:, t[0] : t[1]] = score
            top = jnp.max(score, axis=0, keepdims=True)
            stats_own[step, 0:1, t[0] : t[1]] = top
            stats_own[step, 1:2, t[0] : t[1]] = jnp.sum(jnp.exp(score - top), axis=0, keepdims=True)
        mine = stats_own.at[step, :, pl.ds(0, end)]
        for r in (2, 3, 1):
            send(
                mine,
                stats.at[step, r - 1, :, pl.ds(0, end)],
                s_send.at[step, r - 1],
                s_recv.at[step, r - 1],
                flip[r],
            )
        for r in (1, 2, 3):
            arrived(stats.at[step, r - 1, :, pl.ds(0, end)], s_recv.at[step, r - 1])
        for t in span_all:
            cut = slice(t[0], t[1])
            tops = [stats_own[step, 0:1, cut]] + [stats[step, r, 0:1, cut] for r in range(3)]
            sums = [stats_own[step, 1:2, cut]] + [stats[step, r, 1:2, cut] for r in range(3)]
            top = functools.reduce(jnp.maximum, tops)
            sum_all = sum(s * jnp.exp(m - top) for m, s in zip(tops, sums))
            log_assign = p_all[:, cut] - top - jnp.log(sum_all)
            if last:
                out[...] = log_assign.T[:block, :]
            else:
                a_all[:, cut] = jnp.exp(log_assign).astype(jnp.bfloat16)

    for copy in sent:
        copy.wait_send()


def fused(rows, cols, features, weights_init):
    block, bits = features.shape
    part = weights_init.shape[1]
    blocks = rows * cols
    total = block * blocks
    dma = pltpu.SemaphoreType.DMA
    flops = 2 * total * total * (bits + ITERS * part)
    return pl.pallas_call(
        functools.partial(kernel, rows, cols),
        out_shape=jax.ShapeDtypeStruct((block, part), jnp.float32),
        in_specs=[pl.BlockSpec(memory_space=pl.ANY)] * 2,
        out_specs=pl.BlockSpec(memory_space=pltpu.VMEM),
        scratch_shapes=[
            pltpu.VMEM((4, total, bits // 4), jnp.bfloat16),
            pltpu.VMEM((total, part), jnp.bfloat16),
            pltpu.VMEM((total, total), jnp.bfloat16),
            pltpu.VMEM((part, total), jnp.bfloat16),
            pltpu.VMEM((part, total), jnp.float32),
            pltpu.VMEM((total, 1), jnp.float32),
            pltpu.VMEM((1, total), jnp.float32),
            pltpu.VMEM((ITERS, 3, 2, total), jnp.float32),
            pltpu.VMEM((ITERS, 2, total), jnp.float32),
            dma((5,)),
            dma((4, blocks)),
            dma((4, blocks)),
            dma((cols, rows)),
            dma((rows,)),
            dma((rows,)),
            dma((cols, rows)),
            dma((blocks,)),
            dma((ITERS, 3)),
            dma((ITERS, 3)),
        ],
        compiler_params=pltpu.CompilerParams(
            collective_id=0, has_side_effects=True, vmem_limit_bytes=48 * 1024 * 1024
        ),
        cost_estimate=pl.CostEstimate(
            flops=flops, bytes_accessed=4 * block * (bits + part), transcendentals=total * part
        ),
    )(features, weights_init)


def fits(rows, cols, clus, hits, bits, clusters):
    blocks = rows * cols
    if clus != 4 or hits % blocks or hits % 128 or bits % 512 or clusters % 512:
        return False
    block = hits // blocks
    held = 2 * hits * (bits + hits) + 10 * hits * (clusters // clus)
    return block % 16 == 0 and rows > 1 and cols > 1 and held <= 16 * 1024 * 1024


def solution(mesh):
    placed = (P(("row", "col"), None), P(("row", "col"), "clu"))
    rows, cols, clus = (mesh.shape[a] for a in ("row", "col", "clu"))

    def whole(features, weights_init):
        hits, bits = features.shape
        ok = fits(rows, cols, clus, hits, bits, weights_init.shape[1])
        body = functools.partial(fused, rows, cols) if ok else on_device
        return jax.shard_map(
            body, mesh=mesh, in_specs=placed, out_specs=P(("row", "col"), "clu"), check_vma=False
        )(features, weights_init)

    return whole
```

```python
import functools

import jax
import jax.numpy as jnp
from jax import lax
from jax.experimental import pallas as pl
from jax.experimental.pallas import tpu as pltpu
from jax.sharding import PartitionSpec as P

ITERS = 2


BETA = 320.0


def squared_norms(rows):
    widened = rows.astype(jnp.float32)
    return jnp.sum(widened * widened, axis=1)


def tanimoto(left, left_norms, right):
    gram = jnp.dot(left, right.T, preferred_element_type=jnp.float32)
    return (gram / (left_norms[:, None] + squared_norms(right)[None, :] - gram)).astype(
        jnp.bfloat16
    )


def on_device(features, weights_init):
    references = lax.all_gather(features, "row", axis=0, tiled=True)
    ref_norms = squared_norms(references)
    assign = weights_init
    log_assign = jnp.zeros(weights_init.shape, jnp.float32)
    for step in range(ITERS):
        moving = assign
        kernel_tile = tanimoto(
            references, ref_norms, lax.all_gather(features, "col", axis=0, tiled=True)
        )
        wide_partial = jnp.dot(
            kernel_tile,
            lax.all_gather(moving, "col", axis=0, tiled=True),
            preferred_element_type=jnp.float32,
        )
        products = lax.psum_scatter(wide_partial, "row", scatter_dimension=0, tiled=True)
        widened = assign.astype(jnp.float32)
        local_within = jnp.sum(widened * products, axis=0)
        size_sum, within = lax.psum((jnp.sum(widened, axis=0), local_within), ("row", "col"))
        size_sum = jnp.maximum(size_sum, 1.0)
        score = BETA * (
            2.0 * products / size_sum[None, :] - (within / (size_sum * size_sum))[None, :]
        )
        top = lax.pmax(jnp.max(score, axis=1), "clu")
        total = lax.psum(jnp.sum(jnp.exp(score - top[:, None]), axis=1), "clu")
        log_assign = score - top[:, None] - jnp.log(total)[:, None]
        assign = jnp.exp(log_assign).astype(jnp.bfloat16)
    return log_assign


def block_order(rows, cols):
    near = [dz for dz in range(1, rows) if dz in (1, rows - 1)]
    far = [dz for dz in range(1, rows) if dz not in near]
    order = [(0, 0)] + [(0, dz) for dz in near]
    order += [(dx, 0) for dx in range(1, cols)]
    order += [(0, dz) for dz in far]
    order += [(dx, dz) for dz in near + far for dx in range(1, cols)]
    return order


def strips_after(blocks, block, total):
    done, plan = 0, {}
    for n in range(1, blocks + 1):
        ready = n * block
        grain = 256 if n < blocks - 1 else 128
        end = total if n == blocks else ready // grain * grain
        if end > done:
            plan[n] = (done, end)
            done = end
    return plan


def tiles_of(lo, hi, size=256):
    return [(a, min(a + size, hi)) for a in range(lo, hi, size)]


def kernel(
    rows,
    cols,
    feat,
    weights,
    out,
    f_all,
    w_all,
    k_all,
    a_all,
    p_all,
    norm_col,
    norm_row,
    stats,
    stats_own,
    local_sem,
    f_send,
    f_recv,
    fx_send,
    fz_send,
    w_send,
    wx_send,
    w_recv,
    s_send,
    s_recv,
):
    block = feat.shape[0]
    total, part = w_all.shape
    quarter = f_all.shape[2]
    blocks = rows * cols
    z, x, q = lax.axis_index("row"), lax.axis_index("col"), lax.axis_index("clu")
    y, c = q // 2, q % 2
    order = block_order(rows, cols)
    place = {b: i for i, b in enumerate(order)}

    def row_peer(d):
        return {"row": lax.rem(z + d, rows)}

    def col_peer(d):
        return {"col": lax.rem(x + d, cols)}

    flip = [None, {"clu": y * 2 + 1 - c}, {"clu": (1 - y) * 2 + c}, {"clu": (1 - y) * 2 + 1 - c}]

    def span(i):
        return pl.ds(i * block, block)

    def quarter_of(r):
        index = q if r == 0 else flip[r]["clu"]
        return feat.at[:, pl.ds(pl.multiple_of(index * quarter, quarter), quarter)]

    own = []
    for r in range(4):
        own.append(
            pltpu.make_async_copy(quarter_of(r), f_all.at[r, span(0)], local_sem.at[r])
        )
    own.append(pltpu.make_async_copy(weights, w_all.at[span(0)], local_sem.at[4]))
    for copy in own:
        copy.start()

    barrier = pltpu.get_barrier_semaphore()
    peers = [row_peer(d) for d in range(1, rows)] + [col_peer(d) for d in range(1, cols)] + flip[1:]
    for peer in peers:
        pl.semaphore_signal(barrier, inc=1, device_id=peer, device_id_type=pl.DeviceIdType.MESH)
    pl.semaphore_wait(barrier, len(peers))

    sent = []

    def send(src, dst, send_sem, recv_sem, peer):
        copy = pltpu.make_async_remote_copy(
            src_ref=src,
            dst_ref=dst,
            send_sem=send_sem,
            recv_sem=recv_sem,
            device_id=peer,
            device_id_type=pl.DeviceIdType.MESH,
        )
        copy.start()
        sent.append(copy)

    def arrived(dst, recv_sem):
        pltpu.make_async_copy(dst, dst, recv_sem).wait()

    def send_f_col(b, src):
        for d in range(1, cols):
            i = place[(cols - d, b[1])]
            send(src, f_all.at[0, span(i)], fx_send.at[d, b[1]], f_recv.at[0, i], col_peer(d))

    def send_w_col(b, src):
        for d in range(1, cols):
            i = place[(cols - d, b[1])]
            send(src, w_all.at[span(i)], wx_send.at[d, b[1]], w_recv.at[i], col_peer(d))

    send_f_col((0, 0), quarter_of(0))
    for b in order[1:]:
        if b[0] == 0:
            i = place[(0, rows - b[1])]
            send(quarter_of(0), f_all.at[0, span(i)], fz_send.at[b[1]], f_recv.at[0, i], row_peer(b[1]))

    def send_w_row(near):
        for dz in range(1, rows):
            if (dz in (1, rows - 1)) == near:
                j = place[(0, rows - dz)]
                send(weights, w_all.at[span(j)], w_send.at[dz], w_recv.at[j], row_peer(dz))

    for i, b in enumerate(order):
        here = f_all.at[0, span(i)]
        if i > 0:
            arrived(here, f_recv.at[0, i])
            if b[0] == 0:
                send_f_col(b, here)
            send(here, f_all.at[2, span(i)], f_send.at[2, i], f_recv.at[2, i], flip[2])
            send(here, f_all.at[1, span(i)], f_send.at[1, i], f_recv.at[1, i], flip[1])
        if i == 1:
            send_w_row(True)
        if i == 2:
            send_w_row(False)
        if i == 0:
            send_w_col((0, 0), weights)

    def pass_weights():
        for i, b in enumerate(order):
            if i > 0 and b[0] == 0:
                here = w_all.at[span(i)]
                arrived(here, w_recv.at[i])
                send_w_col(b, here)

    def gram(a, b):
        acc = None
        for r in range(4):
            g = lax.dot_general(
                f_all[r, a[0] : a[1]],
                f_all[r, b[0] : b[1]],
                (((1,), (1,)), ((), ())),
                preferred_element_type=jnp.float32,
            )
            acc = g if acc is None else acc + g
        return acc

    def ratio(g, a, b):
        under = norm_col[a[0] : a[1], :] + norm_row[:, b[0] : b[1]] - g
        return (g / under).astype(jnp.bfloat16)

    def strip(lo, hi):
        for t in tiles_of(lo, hi):
            g = gram(t, t)
            eye = lax.broadcasted_iota(jnp.int32, g.shape, 0) == lax.broadcasted_iota(
                jnp.int32, g.shape, 1
            )
            diag = jnp.where(eye, g, 0.0)
            norm_col[t[0] : t[1], :] = jnp.sum(diag, axis=1, keepdims=True)
            norm_row[:, t[0] : t[1]] = jnp.sum(diag, axis=0, keepdims=True)
            k_all[t[0] : t[1], t[0] : t[1]] = ratio(g, t, t)
            for u in tiles_of(0, t[0]):
                k_all[u[0] : u[1], t[0] : t[1]] = ratio(gram(u, t), u, t)
                k_all[t[0] : t[1], u[0] : u[1]] = ratio(gram(t, u), t, u)

    plan = strips_after(blocks, block, total)
    for copy in own[:4]:
        copy.wait()

    def finish(i):
        for r in (1, 3):
            if i > 0:
                arrived(f_all.at[r, span(i)], f_recv.at[r, i])
        if i + 1 in plan:
            strip(*plan[i + 1])

    for i in range(1, blocks):
        here = f_all.at[2, span(i)]
        arrived(here, f_recv.at[2, i])
        send(here, f_all.at[3, span(i)], f_send.at[3, i], f_recv.at[3, i], flip[1])
        finish(i - 1)
        if i == min(3, blocks - 1):
            pass_weights()
    finish(blocks - 1)

    own[4].wait()
    for i, b in enumerate(order):
        if b[0] > 0:
            arrived(w_all.at[span(i)], w_recv.at[i])
    for t in tiles_of(0, total, 128):
        a_all[:, t[0] : t[1]] = w_all[t[0] : t[1], :].astype(jnp.float32).T.astype(jnp.bfloat16)

    wide = tiles_of(0, total, 384)
    for step in range(ITERS):
        last = step == ITERS - 1
        size = jnp.zeros((part, 1), jnp.float32)
        within = jnp.zeros((part, 1), jnp.float32)
        for t in wide:
            p = jnp.dot(a_all[...], k_all[:, t[0] : t[1]], preferred_element_type=jnp.float32)
            p_all[:, t[0] : t[1]] = p
            a = a_all[:, t[0] : t[1]].astype(jnp.float32)
            size += jnp.sum(a, axis=1, keepdims=True)
            within += jnp.sum(a * p, axis=1, keepdims=True)
        size = jnp.maximum(size, 1.0)
        scale = (2.0 * BETA) / size
        shift = BETA * (within / (size * size))
        span_all = [(0, -(-block // 128) * 128)] if last else wide
        for n, t in enumerate(span_all):
            score = p_all[:, t[0] : t[1]] * scale - shift
            p_all[:, t[0] : t[1]] = score
            top = jnp.max(score, axis=0, keepdims=True)
            stats_own[step, 0:1, t[0] : t[1]] = top
            stats_own[step, 1:2, t[0] : t[1]] = jnp.sum(jnp.exp(score - top), axis=0, keepdims=True)
            cells = pl.ds(t[0], t[1] - t[0])
            for r in (2, 3, 1):
                send(
                    stats_own.at[step, :, cells],
                    stats.at[step, r - 1, :, cells],
                    s_send.at[step, n, r - 1],
                    s_recv.at[step, n, r - 1],
                    flip[r],
                )
        for n, t in enumerate(span_all):
            cells = pl.ds(t[0], t[1] - t[0])
            for r in (1, 2, 3):
                arrived(stats.at[step, r - 1, :, cells], s_recv.at[step, n, r - 1])
            cut = slice(t[0], t[1])
            tops = [stats_own[step, 0:1, cut]] + [stats[step, r, 0:1, cut] for r in range(3)]
            sums = [stats_own[step, 1:2, cut]] + [stats[step, r, 1:2, cut] for r in range(3)]
            top = functools.reduce(jnp.maximum, tops)
            sum_all = sum(s * jnp.exp(m - top) for m, s in zip(tops, sums))
            log_assign = p_all[:, cut] - top - jnp.log(sum_all)
            if last:
                out[...] = log_assign.T[:block, :]
            else:
                a_all[:, cut] = jnp.exp(log_assign).astype(jnp.bfloat16)

    for copy in sent:
        copy.wait_send()


def fused(rows, cols, features, weights_init):
    block, bits = features.shape
    part = weights_init.shape[1]
    blocks = rows * cols
    total = block * blocks
    dma = pltpu.SemaphoreType.DMA
    flops = 2 * total * total * (bits + ITERS * part)
    return pl.pallas_call(
        functools.partial(kernel, rows, cols),
        out_shape=jax.ShapeDtypeStruct((block, part), jnp.float32),
        in_specs=[pl.BlockSpec(memory_space=pl.ANY)] * 2,
        out_specs=pl.BlockSpec(memory_space=pltpu.VMEM),
        scratch_shapes=[
            pltpu.VMEM((4, total, bits // 4), jnp.bfloat16),
            pltpu.VMEM((total, part), jnp.bfloat16),
            pltpu.VMEM((total, total), jnp.bfloat16),
            pltpu.VMEM((part, total), jnp.bfloat16),
            pltpu.VMEM((part, total), jnp.float32),
            pltpu.VMEM((total, 1), jnp.float32),
            pltpu.VMEM((1, total), jnp.float32),
            pltpu.VMEM((ITERS, 3, 2, total), jnp.float32),
            pltpu.VMEM((ITERS, 2, total), jnp.float32),
            dma((5,)),
            dma((4, blocks)),
            dma((4, blocks)),
            dma((cols, rows)),
            dma((rows,)),
            dma((rows,)),
            dma((cols, rows)),
            dma((blocks,)),
            dma((ITERS, len(tiles_of(0, total, 384)), 3)),
            dma((ITERS, len(tiles_of(0, total, 384)), 3)),
        ],
        compiler_params=pltpu.CompilerParams(
            collective_id=0, has_side_effects=True, vmem_limit_bytes=48 * 1024 * 1024
        ),
        cost_estimate=pl.CostEstimate(
            flops=flops, bytes_accessed=4 * block * (bits + part), transcendentals=total * part
        ),
    )(features, weights_init)


def fits(rows, cols, clus, hits, bits, clusters):
    blocks = rows * cols
    if clus != 4 or hits % blocks or hits % 128 or bits % 512 or clusters % 512:
        return False
    block = hits // blocks
    held = 2 * hits * (bits + hits) + 10 * hits * (clusters // clus)
    return block % 16 == 0 and rows > 1 and cols > 1 and held <= 16 * 1024 * 1024


def solution(mesh):
    placed = (P(("row", "col"), None), P(("row", "col"), "clu"))
    rows, cols, clus = (mesh.shape[a] for a in ("row", "col", "clu"))

    def whole(features, weights_init):
        hits, bits = features.shape
        ok = fits(rows, cols, clus, hits, bits, weights_init.shape[1])
        body = functools.partial(fused, rows, cols) if ok else on_device
        return jax.shard_map(
            body, mesh=mesh, in_specs=placed, out_specs=P(("row", "col"), "clu"), check_vma=False
        )(features, weights_init)

    return whole
```
